256 devices in a mesh: ctx: 128 (over x, y, z), head: 2 (over core).
Axes of the slice: x: 4, y: 4, z: 8, core: 2. Of those that a mesh axis runs over, the one named last changes fastest.
Arguments:
- tokens: bfloat16 [65536, 2048], P('ctx', 'head'), may hold values from -6 to 6
- w_query: bfloat16 [2048, 256], P(None, 'head'), may hold values from -0.125 to 0.125
- w_key: bfloat16 [2048, 256], P(None, 'head'), may hold values from -0.125 to 0.125
- w_value: bfloat16 [2048, 2048], P(None, 'head'), may hold values from -0.125 to 0.125
- conv_query: bfloat16 [3, 256], P(None, 'head'), may hold values from -3 to 3
- conv_key: bfloat16 [3, 256], P(None, 'head'), may hold values from -3 to 3
- conv_value: bfloat16 [3, 2048], P(None, 'head'), may hold values from -3 to 3
- w_out: bfloat16 [2048, 2048], P('head'), may hold values from -1.3258252 to 1.3258252
- gain: bfloat16 [2048], P('head'), may hold values from 0.099609375 to 1.8984375
Outputs:
- mixed: bfloat16 [65536, 2048], P('ctx', 'head')
The draws below stay inside these ranges and needn't reach their ends.
All inputs are finite; a program needn't handle non-finite values.
Results may differ from the reference program's by a relative error of at most 0.011.
Values may be sent and summed in bfloat16 or wider, within the bound.
A program may use at most 192 MiB of HBM per device.

```python
import math
import jax
import jax.numpy as jnp
from jax import lax

D = 2048
HEADS = 16
FD = 16
DV = 128
KCONV = 3
TOK_DEV = 512
FEAT = 153
TOKENS = 65536
N_CTX = 128


def draw_w_out(key, part):
    first, second = jax.random.split(key)
    base = jnp.clip(jax.random.normal(first, (HEADS * DV, D), jnp.float32), -6.0, 6.0)
    columns = jnp.exp(jax.random.uniform(second, (1, D), jnp.float32, 0.0, math.log(10.0)))
    return (base * columns / math.sqrt(HEADS * DV)).astype(jnp.bfloat16)


def level_of(stream_key, extent, cuts, smallest, high):
    def one(axis_at, blocks):
        steps = jax.random.uniform(jax.random.fold_in(jax.random.fold_in(stream_key, 6), axis_at), (blocks,), jnp.float32, smallest / len(cuts), high / len(cuts))
        return jnp.repeat(jnp.exp(steps), extent[axis_at] // blocks).reshape((-1,) + (1,) * (len(extent) - axis_at - 1))

    factor_of = one(*cuts[0])
    for cut in cuts[1:]:
        factor_of = factor_of * one(*cut)
    return factor_of


def noise(rng, dims, spread, bound, shards=(), held_as=jnp.bfloat16):
    level = level_of(rng, dims, shards, -0.22, 0.18) if shards else 1.0
    array = jax.random.normal(rng, dims, jnp.float32) * spread * level
    return jnp.minimum(jnp.maximum(array, -bound), bound).astype(held_as)


def setup_inputs(seed: int = 0) -> dict:
    arg_keys = jax.random.split(jax.random.key(seed), 10)
    tokens = noise(arg_keys[0], (TOKENS, D), 1.0, 6.0, ((0, 128), (1, 2)))
    w_query = noise(arg_keys[1], (D, HEADS * FD), D ** -0.5, 0.125, ((1, 2),))
    w_key = noise(arg_keys[2], (D, HEADS * FD), D ** -0.5, 0.125, ((1, 2),))
    w_value = noise(arg_keys[3], (D, HEADS * DV), D ** -0.5, 0.125, ((1, 2),))
    conv_query = noise(arg_keys[4], (KCONV, HEADS * FD), 0.6, 3.0, ((1, 2),))
    conv_key = noise(arg_keys[5], (KCONV, HEADS * FD), 0.6, 3.0, ((1, 2),))
    conv_value = noise(arg_keys[6], (KCONV, HEADS * DV), 0.6, 3.0, ((1, 2),))
    w_out = draw_w_out(jax.random.fold_in(arg_keys[9], 71), 0)
    gain = jnp.clip(1.0 + 0.18 * jax.random.normal(arg_keys[8], (D,), jnp.float32), 0.099609375, 1.8984375).astype(jnp.bfloat16)
    return dict(tokens=tokens, w_query=w_query, w_key=w_key, w_value=w_value, conv_query=conv_query, conv_key=conv_key, conv_value=conv_value, w_out=w_out, gain=gain)


def taylor_features(u):
    width = u.shape[-1]
    pieces = [jnp.ones(u.shape[:-1] + (1,), jnp.float32), u * width ** (-0.25)]
    for index in range(width):
        scales = jnp.concatenate([jnp.full((1,), 1.0 / math.sqrt(2.0 * width), jnp.float32), jnp.full((width - index - 1,), 1.0 / math.sqrt(width), jnp.float32)])
        pieces.append(u[..., index:index + 1] * u[..., index:] * scales)
    return jnp.concatenate(pieces, -1)

def causal_conv(projected, taps):
    padded = jnp.concatenate([jnp.zeros((2, projected.shape[1]), projected.dtype), projected], 0).astype(jnp.float32)
    tapf = taps.astype(jnp.float32)
    length = projected.shape[0]
    return tapf[0] * padded[2:2 + length] + tapf[1] * padded[1:1 + length] + tapf[2] * padded[0:length]

def reference(tokens, w_query, w_key, w_value, conv_query, conv_key, conv_value, w_out, gain):
    hp = lax.Precision.HIGHEST
    qp = jnp.dot(tokens, w_query, preferred_element_type=jnp.float32).astype(jnp.bfloat16)
    kp = jnp.dot(tokens, w_key, preferred_element_type=jnp.float32).astype(jnp.bfloat16)
    vp = jnp.dot(tokens, w_value, preferred_element_type=jnp.float32).astype(jnp.bfloat16)
    query = causal_conv(qp, conv_query).reshape(TOKENS, HEADS, FD)
    keyed = causal_conv(kp, conv_key).reshape(TOKENS, HEADS, FD)
    values = causal_conv(vp, conv_value).astype(jnp.bfloat16).reshape(N_CTX, TOK_DEV, HEADS, DV)
    pq = taylor_features(query).astype(jnp.bfloat16).reshape(N_CTX, TOK_DEV, HEADS, FEAT)
    pk = taylor_features(keyed).astype(jnp.bfloat16).reshape(N_CTX, TOK_DEV, HEADS, FEAT)
    causal = jnp.arange(TOK_DEV)[:, None] >= jnp.arange(TOK_DEV)[None, :]
    gainf = gain.astype(jnp.float32)

    def span_step(carry, inputs):
        state, normer = carry
        bq, bk, bv = inputs
        pqf = bq.astype(jnp.float32)
        pkf = bk.astype(jnp.float32)
        vf = bv.astype(jnp.float32)
        scores = jnp.einsum('thf,shf->hts', pqf, pkf, precision=hp)
        scores = jnp.where(causal[None], scores, jnp.float32(0.0))
        rounded = scores.astype(jnp.bfloat16).astype(jnp.float32)
        numer = jnp.einsum('hts,shd->thd', rounded, vf, precision=hp) + jnp.einsum('thf,hfd->thd', pqf, state, precision=hp)
        denom = lax.optimization_barrier(jnp.sum(scores, -1)).T + jnp.einsum('thf,hf->th', pqf, normer, precision=hp)
        mixed_heads = (numer / denom[:, :, None]).astype(jnp.bfloat16).reshape(TOK_DEV, HEADS * DV)
        pre = jnp.dot(mixed_heads, w_out, preferred_element_type=jnp.float32)
        scale = lax.rsqrt(lax.optimization_barrier(jnp.mean(pre * pre, -1, keepdims=True)) + 1e-05)
        result = (pre * scale * gainf).astype(jnp.bfloat16)
        state = state + jnp.einsum('shf,shd->hfd', pkf, vf, precision=hp)
        normer = normer + lax.optimization_barrier(jnp.sum(pkf, 0))
        return ((state, normer), result)
    start = (jnp.zeros((HEADS, FEAT, DV), jnp.float32), jnp.zeros((HEADS, FEAT), jnp.float32))
    final, outputs = lax.scan(span_step, start, (pq, pk, values))
    return outputs.reshape(TOKENS, D)
```

```python
import math

import jax
import jax.numpy as jnp
from jax import lax
from jax.experimental import pallas as pl
from jax.experimental.pallas import tpu as pltpu
from jax.sharding import PartitionSpec as P

D = 2048
HALF = 1024
FD = 16
DV = 128
ROWS = 512
HALO = 16
PADDED = HALO + ROWS
HEADS = 8
FEAT = 160
TILE = 256
Z, Y, X = 8, 4, 4
BF = jnp.bfloat16
F32 = jnp.float32
MESH = pl.DeviceIdType.MESH
PAIR_ORDER = (2, 1, 3, 0)
Z_ORDER = (4, 3, 5, 2, 6, 1, 7)


def dot(a, b):
    return jnp.dot(a, b, preferred_element_type=F32)


def features(u):
    parts = [u * u * F32(1.0 / math.sqrt(2.0 * FD))]
    for distance in range(1, 8):
        parts.append(u * pltpu.roll(u, FD - distance, 0) * F32(1.0 / math.sqrt(FD)))
    parts.append(u[0:8] * u[8:16] * F32(1.0 / math.sqrt(FD)))
    parts.append(u * F32(FD ** (-0.25)))
    row = lax.broadcasted_iota(jnp.int32, (8, u.shape[1]), 0)
    parts.append(jnp.where(row == 0, F32(1.0), F32(0.0)))
    return jnp.concatenate(parts, 0)


def kernel(
    tok, wq, wk, wv, cq, ck, cv, wo, gn, out,
    xbuf, wqk, wvb, wob, cqb, ckb, cvb, gnb,
    acc, pbuf, qt, kt, vbuf, pk, pq, num,
    loc, recv1, cbuf, ltx, ry, ttx, rx, p3, recv3,
    ybuf, ttxo, trx, share, sqtx, sqrx, obuf,
    lsem, tok_s, tok_r, halo_s, halo_r, s1_s, s1_r, y_s, y_r, x_s, x_r, s3_s, s3_r, o_s, o_r, q_s, q_r,
):
    me = lax.axis_index("ctx")
    c = lax.axis_index("head")
    other = 1 - c
    z = lax.rem(me, Z)
    y = lax.rem(lax.div(me, Z), Y)
    x = lax.div(me, Z * Y)

    def z_peer(i):
        return me - z + lax.rem(z + i, Z)

    def y_peer(i):
        return me + (lax.rem(y + i, Y) - y) * Z

    def x_peer(i):
        return me + (lax.rem(x + i, X) - x) * (Z * Y)

    after = lax.rem(me + 1, Z * Y * X)
    before = lax.rem(me + Z * Y * X - 1, Z * Y * X)

    def remote(src, dst, send, recv, ctx, head):
        return pltpu.make_async_remote_copy(
            src_ref=src, dst_ref=dst, send_sem=send, recv_sem=recv,
            device_id={"ctx": ctx, "head": head}, device_id_type=MESH,
        )

    barrier = pltpu.get_barrier_semaphore()
    greeted = [(me, other), (before, c), (before, other)]
    greeted += [(z_peer(i), c) for i in range(1, Z)]
    greeted += [(y_peer(i), c) for i in range(1, Y)]
    greeted += [(x_peer(i), c) for i in range(1, X)]
    for ctx, head in greeted:
        pl.semaphore_signal(barrier, inc=1, device_id={"ctx": ctx, "head": head}, device_id_type=MESH)

    mine = pl.ds(pl.multiple_of(c * HALF, HALF), HALF)
    theirs = pl.ds(pl.multiple_of(other * HALF, HALF), HALF)
    tail_rows = pl.ds(HALO, ROWS)
    loads = [
        pltpu.make_async_copy(tok, xbuf.at[c, tail_rows], lsem.at[0]),
        pltpu.make_async_copy(wq, wqk.at[:, pl.ds(0, 128)], lsem.at[1]),
        pltpu.make_async_copy(wk, wqk.at[:, pl.ds(128, 128)], lsem.at[2]),
        pltpu.make_async_copy(wv.at[mine], wvb.at[mine], lsem.at[3]),
        pltpu.make_async_copy(wv.at[theirs], wvb.at[theirs], lsem.at[4]),
        pltpu.make_async_copy(cq, cqb, lsem.at[5]),
        pltpu.make_async_copy(ck, ckb, lsem.at[6]),
        pltpu.make_async_copy(cv, cvb, lsem.at[7]),
        pltpu.make_async_copy(gn, gnb, lsem.at[8]),
        pltpu.make_async_copy(wo, wob, lsem.at[9]),
    ]
    for copy in loads:
        copy.start()
    pl.semaphore_wait(barrier, len(greeted))

    last = tok.at[pl.ds(ROWS - HALO, HALO)]
    halos = [
        remote(last, xbuf.at[c, pl.ds(0, HALO)], halo_s.at[0], halo_r.at[c], after, c),
        remote(last, xbuf.at[c, pl.ds(0, HALO)], halo_s.at[1], halo_r.at[c], after, other),
    ]
    swap = remote(tok, xbuf.at[c, tail_rows], tok_s.at[0], tok_r.at[0], me, other)
    for copy in halos:
        copy.start()
    swap.start()

    def halo_in(half):
        remote(last, xbuf.at[half, pl.ds(0, HALO)], halo_s.at[0], halo_r.at[half], before, c).wait_recv()

    halo_in(c)
    for copy in loads[:4]:
        copy.wait()

    def columns(pair):
        return pl.ds(pl.multiple_of(pair * TILE, TILE), TILE)

    pairs = [lax.rem(lax.div(z, 2) + i, 4) for i in PAIR_ORDER]
    acc[0] = dot(xbuf[c], wqk[mine, :])
    for i, pair in enumerate(pairs):
        acc[1 + i] = dot(xbuf[c], wvb[mine, columns(pair)])
    halo_in(other)
    swap.wait_recv()
    for copy in loads[4:]:
        copy.wait()

    first_block = me == 0

    def convolved(taps):
        pbuf[8:16, :] = jnp.where(first_block, F32(0.0), pbuf[8:16, :])
        return (
            taps[0:1] * pbuf[16 : 16 + ROWS, :]
            + taps[1:2] * pbuf[15 : 15 + ROWS, :]
            + taps[2:3] * pbuf[14 : 14 + ROWS, :]
        )

    pbuf[...] = (acc[0] + dot(xbuf[other], wqk[theirs, :])).astype(BF).astype(F32)
    taps = jnp.concatenate([cqb[...].astype(F32), ckb[...].astype(F32)], 1)
    both = convolved(taps).T
    qt[...] = both[0:128]
    kt[...] = both[128:256]

    def key_head(h, value):
        feats = features(kt[pl.ds(pl.multiple_of(h * FD, FD), FD), :]).astype(BF)
        pk[h] = feats
        state = dot(feats, value)
        norm = lax.dot_general(
            jnp.ones((8, ROWS), BF), feats, (((1,), (1,)), ((), ())), preferred_element_type=F32
        )[0:1]
        norm = jnp.concatenate([norm, jnp.zeros((1, 256 - FEAT), F32)], 1)
        row = lax.broadcasted_iota(jnp.int32, (16, DV), 0)
        tail = state[144:160]
        tail = jnp.where(row == 9, norm[:, 0:128], tail)
        tail = jnp.where(row == 10, norm[:, 128:256], tail)
        return jnp.concatenate([state[0:144], tail], 0).astype(BF)

    sends1 = []
    for i, pair in enumerate(pairs):
        pbuf[...] = (acc[1 + i] + dot(xbuf[other], wvb[theirs, columns(pair)])).astype(BF).astype(F32)
        values = convolved(cvb[:, columns(pair)].astype(F32)).astype(BF)
        vbuf[pair] = values
        if PAIR_ORDER[i]:
            for b in range(2):
                slot = 2 * i + b
                loc[slot] = key_head(2 * pair + b, values[:, b * DV : (b + 1) * DV])
                sends1.append((slot, 2 * pair + b))
                slot, dest = sends1[-1]
                remote(loc.at[slot], recv1.at[z], s1_s.at[slot], s1_r.at[z], me - z + dest, c).start()
        else:
            half = lax.rem(z, 2)
            dest = 2 * pair + (1 - half)
            slot = 2 * i
            chosen = jnp.where(half == 0, values[:, DV:], values[:, :DV])
            loc[slot] = key_head(dest, chosen)
            sends1.append((slot, dest))
            remote(loc.at[slot], recv1.at[z], s1_s.at[slot], s1_r.at[z], me - z + dest, c).start()
            chosen = jnp.where(half == 0, values[:, :DV], values[:, DV:])
            recv1[z] = key_head(z, chosen)

    ones = jnp.ones((ROWS, DV), BF)

    def query_head(h):
        feats = features(qt[h * FD : (h + 1) * FD, :])
        pq[h] = jnp.concatenate([feats, jnp.zeros((256 - FEAT, ROWS), F32)], 0).T.astype(BF)
        value = vbuf[h // 2][:, (h % 2) * DV : (h % 2 + 1) * DV]
        value = jnp.concatenate([value, ones], 1)
        for t in range(ROWS // TILE):
            span = (t + 1) * TILE
            scores = dot(pq[h, t * TILE : span, 0:FEAT], pk[h, :, 0:span])
            row = lax.broadcasted_iota(jnp.int32, (TILE, span), 0) + t * TILE
            col = lax.broadcasted_iota(jnp.int32, (TILE, span), 1)
            scores = jnp.where(row >= col, scores, F32(0.0)).astype(BF)
            num[h, t * TILE : span] = dot(scores, value[0:span])

    for h in range(3):
        query_head(h)

    for i in range(1, Z):
        slot = lax.rem(z + Z - i, Z)
        remote(loc.at[0], recv1.at[slot], s1_s.at[0], s1_r.at[slot], z_peer(i), c).wait_recv()
    total = jnp.zeros((FEAT, DV), F32)
    for t in range(Z):
        cbuf[t] = total
        total = total + recv1[t].astype(F32)
    line = total.astype(BF)
    ltx[...] = line
    sends_y = [remote(ltx, ry.at[y], y_s.at[i], y_r.at[y], y_peer(i), c) for i in range(1, Y)]
    for copy in sends_y:
        copy.start()
    ry[y] = line

    for h in range(3, 5):
        query_head(h)

    for i in range(1, Y):
        slot = lax.rem(y + Y - i, Y)
        remote(ltx, ry.at[slot], y_s.at[0], y_r.at[slot], y_peer(i), c).wait_recv()
    offset = jnp.zeros((FEAT, DV), F32)
    total = jnp.zeros((FEAT, DV), F32)
    for t in range(Y):
        part = ry[t].astype(F32)
        total = total + part
        offset = offset + jnp.where(t < y, part, F32(0.0))
    plane = total.astype(BF)
    ttx[...] = plane
    sends_x = [remote(ttx, rx.at[x], x_s.at[i], x_r.at[x], x_peer(i), c) for i in range(1, X)]
    for copy in sends_x:
        copy.start()
    rx[x] = plane

    for h in range(5, 8):
        query_head(h)

    for i in range(1, X):
        slot = lax.rem(x + X - i, X)
        remote(ttx, rx.at[slot], x_s.at[0], x_r.at[slot], x_peer(i), c).wait_recv()
    for t in range(X):
        offset = offset + jnp.where(t < x, rx[t].astype(F32), F32(0.0))
    sends3 = []
    for i in Z_ORDER:
        dest = lax.rem(z + i, Z)
        p3[i] = (cbuf[dest] + offset).astype(BF)
        sends3.append(remote(p3.at[i], recv3.at[z], s3_s.at[i], s3_r.at[z], me - z + dest, c))
        sends3[-1].start()
    recv3[z] = (cbuf[z] + offset).astype(BF)

    def finish_head(h):
        state = recv3[h]
        tail = state[144:160].astype(F32)
        norm = jnp.concatenate([tail[9:10], tail[10:11]], 1)
        norm = jnp.broadcast_to(norm, (128, 256)).T[0:FEAT].astype(BF)
        sums = dot(pq[h][:, 0:FEAT], jnp.concatenate([state, norm], 1)) + num[h]
        ybuf[:, pl.ds(pl.multiple_of(h * DV, DV), DV)] = (sums[:, :DV] / sums[:, DV:]).astype(BF)

    finish_head(z)
    for i in Z_ORDER:
        slot = lax.rem(z + Z - i, Z)
        remote(p3.at[i], recv3.at[slot], s3_s.at[i], s3_r.at[slot], z_peer(i), c).wait_recv()
        finish_head(slot)

    sends_o = []
    for n in range(HALF // TILE):
        cols = pl.ds(pl.multiple_of(other * HALF + n * TILE, TILE), TILE)
        ttxo[n] = dot(ybuf[...], wob[:, cols]).astype(BF)
        sends_o.append(remote(ttxo.at[n], trx.at[n], o_s.at[n], o_r.at[n], me, other))
        sends_o[-1].start()
    squares = jnp.zeros((ROWS, 128), F32)
    for n in range(HALF // TILE):
        cols = pl.ds(pl.multiple_of(c * HALF + n * TILE, TILE), TILE)
        term = dot(ybuf[...], wob[:, cols])
        sends_o[n].wait_recv()
        term = term + trx[n].astype(F32)
        share[n] = term
        squares = squares + term[:, :128] * term[:, :128] + term[:, 128:] * term[:, 128:]
    sqtx[...] = squares
    send_q = remote(sqtx, sqrx, q_s.at[0], q_r.at[0], me, other)
    send_q.start()
    send_q.wait_recv()
    mean = jnp.sum(sqtx[...] + sqrx[...], 1, keepdims=True) * F32(1.0 / D)
    scale = lax.rsqrt(mean + F32(1e-05))
    stores = []
    for n in range(HALF // TILE):
        cols = pl.ds(n * TILE, TILE)
        obuf[:, cols] = (share[n] * scale * gnb[:, cols].astype(F32)).astype(BF)
        stores.append(pltpu.make_async_copy(obuf.at[:, cols], out.at[:, cols], lsem.at[n]))
        stores[-1].start()

    for copy in halos:
        copy.wait_send()
    swap.wait_send()
    for slot, dest in sends1:
        remote(loc.at[slot], recv1.at[z], s1_s.at[slot], s1_r.at[z], me - z + dest, c).wait_send()
    for copy in sends_y + sends_x + sends3 + sends_o + [send_q]:
        copy.wait_send()
    for copy in stores:
        copy.wait()


def body(tokens, w_query, w_key, w_value, conv_query, conv_key, conv_value, w_out, gain):
    dma = pltpu.SemaphoreType.DMA
    vm = pltpu.VMEM
    return pl.pallas_call(
        kernel,
        out_shape=jax.ShapeDtypeStruct((ROWS, HALF), BF),
        in_specs=[pl.BlockSpec(memory_space=pl.ANY)] * 9,
        out_specs=pl.BlockSpec(memory_space=pl.ANY),
        scratch_shapes=[
            vm((2, PADDED, HALF), BF), vm((D, 256), BF), vm((D, HALF), BF), vm((HALF, D), BF),
            vm((3, 128), BF), vm((3, 128), BF), vm((3, HALF), BF), vm((1, HALF), BF),
            vm((5, PADDED, TILE), F32), vm((PADDED, TILE), F32), vm((128, ROWS), F32), vm((128, ROWS), F32),
            vm((4, ROWS, TILE), BF), vm((HEADS, FEAT, ROWS), BF), vm((HEADS, ROWS, 256), BF),
            vm((HEADS, ROWS, TILE), F32),
            vm((8, FEAT, DV), BF), vm((Z, FEAT, DV), BF), vm((Z, FEAT, DV), F32), vm((FEAT, DV), BF),
            vm((Y, FEAT, DV), BF), vm((FEAT, DV), BF), vm((X, FEAT, DV), BF), vm((Z, FEAT, DV), BF),
            vm((Z, FEAT, DV), BF),
            vm((ROWS, HALF), BF), vm((4, ROWS, TILE), BF), vm((4, ROWS, TILE), BF), vm((4, ROWS, TILE), F32),
            vm((ROWS, 128), F32), vm((ROWS, 128), F32), vm((ROWS, HALF), BF),
            dma((10,)), dma((1,)), dma((1,)), dma((2,)), dma((2,)), dma((8,)), dma((8,)), dma((4,)), dma((4,)),
            dma((4,)), dma((4,)), dma((8,)), dma((8,)), dma((4,)), dma((4,)), dma((1,)), dma((1,)),
        ],
        compiler_params=pltpu.CompilerParams(
            collective_id=0, has_side_effects=True, vmem_limit_bytes=58 * 1024 * 1024
        ),
    )(tokens, w_query, w_key, w_value, conv_query, conv_key, conv_value, w_out, gain.reshape(1, HALF))


def solution(mesh):
    return jax.shard_map(
        body,
        mesh=mesh,
        in_specs=(
            P("ctx", "head"),
            P(None, "head"),
            P(None, "head"),
            P(None, "head"),
            P(None, "head"),
            P(None, "head"),
            P(None, "head"),
            P("head", None),
            P("head"),
        ),
        out_specs=P("ctx", "head"),
        check_vma=False,
    )
```

```python
import math

import jax
import jax.numpy as jnp
from jax import lax
from jax.experimental import pallas as pl
from jax.experimental.pallas import tpu as pltpu
from jax.sharding import PartitionSpec as P

D = 2048
HALF = 1024
FD = 16
DV = 128
ROWS = 512
HALO = 16
PADDED = HALO + ROWS
HEADS = 8
FEAT = 160
TILE = 256
Z, Y, X = 8, 4, 4
BF = jnp.bfloat16
F32 = jnp.float32
MESH = pl.DeviceIdType.MESH
PLANE = X * Y
CHUNK = FEAT // 2
PAIR_ORDER = (2, 1, 3, 0)
Z_ORDER = (4, 3, 5, 2, 6, 1, 7)


def dot(a, b):
    return jnp.dot(a, b, preferred_element_type=F32)


def features(u):
    parts = [u * u * F32(1.0 / math.sqrt(2.0 * FD))]
    for distance in range(1, 8):
        parts.append(u * pltpu.roll(u, FD - distance, 0) * F32(1.0 / math.sqrt(FD)))
    parts.append(u[0:8] * u[8:16] * F32(1.0 / math.sqrt(FD)))
    parts.append(u * F32(FD ** (-0.25)))
    row = lax.broadcasted_iota(jnp.int32, (8, u.shape[1]), 0)
    parts.append(jnp.where(row == 0, F32(1.0), F32(0.0)))
    return jnp.concatenate(parts, 0)


def kernel(
    tok, wq, wk, wv, cq, ck, cv, wo, gn, out,
    xbuf, wqk, wvb, wob, cqb, ckb, cvb, gnb,
    acc, pbuf, qt, kt, vbuf, pk, pq, num,
    loc, recv1, cbuf, ltx, lrx, offset, p3, recv3,
    acc_out, ttxo, trx, share, sqtx, sqrx,
    lsem, tok_s, tok_r, halo_s, halo_r, s1_s, s1_r, l_s, l_r, s3_s, s3_r, o_s, o_r, q_s, q_r,
):
    me = lax.axis_index("ctx")
    c = lax.axis_index("head")
    other = 1 - c
    z = lax.rem(me, Z)
    line = lax.div(me, Z)

    def z_peer(i):
        return me - z + lax.rem(z + i, Z)

    def line_peer(i):
        return lax.rem(line + i + PLANE, PLANE) * Z + z

    after = lax.rem(me + 1, Z * Y * X)
    before = lax.rem(me + Z * Y * X - 1, Z * Y * X)

    def remote(src, dst, send, recv, ctx, head):
        return pltpu.make_async_remote_copy(
            src_ref=src, dst_ref=dst, send_sem=send, recv_sem=recv,
            device_id={"ctx": ctx, "head": head}, device_id_type=MESH,
        )

    barrier = pltpu.get_barrier_semaphore()
    greeted = [(me, other), (before, c), (before, other)]
    greeted += [(z_peer(i), c) for i in range(1, Z)]
    greeted += [(line_peer(i), c) for i in range(1, PLANE)]
    for ctx, head in greeted:
        pl.semaphore_signal(barrier, inc=1, device_id={"ctx": ctx, "head": head}, device_id_type=MESH)

    mine = pl.ds(pl.multiple_of(c * HALF, HALF), HALF)
    theirs = pl.ds(pl.multiple_of(other * HALF, HALF), HALF)
    tail_rows = pl.ds(HALO, ROWS)
    loads = [
        pltpu.make_async_copy(tok, xbuf.at[c, tail_rows], lsem.at[0]),
        pltpu.make_async_copy(wq, wqk.at[:, pl.ds(0, 128)], lsem.at[1]),
        pltpu.make_async_copy(wk, wqk.at[:, pl.ds(128, 128)], lsem.at[2]),
        pltpu.make_async_copy(wv.at[mine], wvb.at[mine], lsem.at[3]),
        pltpu.make_async_copy(wv.at[theirs], wvb.at[theirs], lsem.at[4]),
        pltpu.make_async_copy(cq, cqb, lsem.at[5]),
        pltpu.make_async_copy(ck, ckb, lsem.at[6]),
        pltpu.make_async_copy(cv, cvb, lsem.at[7]),
        pltpu.make_async_copy(gn, gnb, lsem.at[8]),
        pltpu.make_async_copy(wo, wob, lsem.at[9]),
    ]
    for copy in loads:
        copy.start()
    pl.semaphore_wait(barrier, len(greeted))

    last = tok.at[pl.ds(ROWS - HALO, HALO)]
    halos = [
        remote(last, xbuf.at[c, pl.ds(0, HALO)], halo_s.at[0], halo_r.at[c], after, c),
        remote(last, xbuf.at[c, pl.ds(0, HALO)], halo_s.at[1], halo_r.at[c], after, other),
    ]
    swap = remote(tok, xbuf.at[c, tail_rows], tok_s.at[0], tok_r.at[0], me, other)
    swap.start()

    @pl.when(me < Z * PLANE - 1)
    def _():
        for copy in halos:
            copy.start()

    def halo_in(half):
        rows = xbuf.at[half, pl.ds(0, HALO)]

        @pl.when(me > 0)
        def _():
            remote(last, rows, halo_s.at[0], halo_r.at[half], before, c).wait_recv()

        @pl.when(me == 0)
        def _():
            rows[...] = jnp.zeros((HALO, HALF), BF)

    halo_in(c)
    for copy in loads[:4]:
        copy.wait()

    def columns(pair):
        return pl.ds(pl.multiple_of(pair * TILE, TILE), TILE)

    pairs = [lax.rem(lax.div(z, 2) + i, 4) for i in PAIR_ORDER]
    acc[0] = dot(xbuf[c], wqk[mine, :])
    for i, pair in enumerate(pairs):
        acc[1 + i] = dot(xbuf[c], wvb[mine, columns(pair)])
    halo_in(other)
    swap.wait_recv()
    for copy in loads[4:]:
        copy.wait()

    def convolved(taps):
        return (
            taps[0:1] * pbuf[16 : 16 + ROWS, :]
            + taps[1:2] * pbuf[15 : 15 + ROWS, :]
            + taps[2:3] * pbuf[14 : 14 + ROWS, :]
        )

    pbuf[...] = (acc[0] + dot(xbuf[other], wqk[theirs, :])).astype(BF).astype(F32)
    taps = jnp.concatenate([cqb[...].astype(F32), ckb[...].astype(F32)], 1)
    both = convolved(taps).T
    qt[...] = both[0:128]
    kt[...] = both[128:256]

    def key_head(h, value):
        feats = features(kt[pl.ds(pl.multiple_of(h * FD, FD), FD), :]).astype(BF)
        pk[h] = feats
        state = dot(feats, value)
        norm = lax.dot_general(
            jnp.ones((8, ROWS), BF), feats, (((1,), (1,)), ((), ())), preferred_element_type=F32
        )[0:1]
        norm = jnp.concatenate([norm, jnp.zeros((1, 256 - FEAT), F32)], 1)
        row = lax.broadcasted_iota(jnp.int32, (16, DV), 0)
        tail = state[144:160]
        tail = jnp.where(row == 9, norm[:, 0:128], tail)
        tail = jnp.where(row == 10, norm[:, 128:256], tail)
        return jnp.concatenate([state[0:144], tail], 0).astype(BF)

    def rows_of(chunk):
        return pl.ds(chunk * CHUNK, CHUNK)

    sends1 = []

    def state_out(slot, dest, chunk):
        rows = rows_of(chunk)
        sends1.append(
            remote(
                loc.at[slot, rows], recv1.at[z, rows], s1_s.at[chunk, slot], s1_r.at[chunk, z], me - z + dest, c
            )
        )
        sends1[-1].start()

    routed = []
    for i, pair in enumerate(pairs):
        pbuf[...] = (acc[1 + i] + dot(xbuf[other], wvb[theirs, columns(pair)])).astype(BF).astype(F32)
        values = convolved(cvb[:, columns(pair)].astype(F32)).astype(BF)
        vbuf[pair] = values
        if PAIR_ORDER[i]:
            for b in range(2):
                slot, dest = 2 * i + b, 2 * pair + b
                loc[slot] = key_head(dest, values[:, b * DV : (b + 1) * DV])
                routed.append((slot, dest))
                state_out(slot, dest, 0)
        else:
            half = lax.rem(z, 2)
            slot, dest = 2 * i, 2 * pair + (1 - half)
            loc[slot] = key_head(dest, jnp.where(half == 0, values[:, DV:], values[:, :DV]))
            routed.append((slot, dest))
            state_out(slot, dest, 0)
    for slot, dest in routed:
        state_out(slot, dest, 1)
    half = lax.rem(z, 2)
    recv1[z] = key_head(z, jnp.where(half == 0, values[:, :DV], values[:, DV:]))

    ones = jnp.ones((ROWS, DV), BF)

    def query_head(h):
        feats = features(qt[h * FD : (h + 1) * FD, :])
        pq[h] = jnp.concatenate([feats, jnp.zeros((256 - FEAT, ROWS), F32)], 0).T.astype(BF)
        value = vbuf[h // 2][:, (h % 2) * DV : (h % 2 + 1) * DV]
        value = jnp.concatenate([value, ones], 1)
        for t in range(ROWS // TILE):
            span = (t + 1) * TILE
            scores = dot(pq[h, t * TILE : span, 0:FEAT], pk[h, :, 0:span])
            row = lax.broadcasted_iota(jnp.int32, (TILE, span), 0) + t * TILE
            col = lax.broadcasted_iota(jnp.int32, (TILE, span), 1)
            scores = jnp.where(row >= col, scores, F32(0.0)).astype(BF)
            num[h, t * TILE : span] = dot(scores, value[0:span])

    def line_send(chunk, i):
        rows = rows_of(chunk)
        return remote(
            ltx.at[rows], lrx.at[i, rows], l_s.at[chunk, i], l_r.at[chunk, i], line_peer(i), c
        )

    def line_totals(chunk):
        rows = rows_of(chunk)
        for i in range(1, Z):
            slot = lax.rem(z + Z - i, Z)
            remote(
                loc.at[0, rows], recv1.at[slot, rows], s1_s.at[chunk, 0], s1_r.at[chunk, slot], z_peer(i), c
            ).wait_recv()
        total = jnp.zeros((CHUNK, DV), F32)
        for t in range(Z):
            cbuf[t, rows] = total
            total = total + recv1[t, rows].astype(F32)
        ltx[rows] = total.astype(BF)
        for i in range(1, PLANE):

            @pl.when(line + i < PLANE)
            def _():
                line_send(chunk, i).start()

    sends3 = []

    def prefixes(chunk):
        rows = rows_of(chunk)
        offset[rows] = jnp.zeros((CHUNK, DV), F32)
        for i in range(1, PLANE):

            @pl.when(line >= i)
            def _():
                line_send(chunk, i).wait_recv()
                offset[rows] += lrx[i, rows].astype(F32)

        for i in Z_ORDER:
            dest = lax.rem(z + i, Z)
            p3[i, rows] = (cbuf[dest, rows] + offset[rows]).astype(BF)
            sends3.append(
                remote(p3.at[i, rows], recv3.at[z, rows], s3_s.at[chunk, i], s3_r.at[chunk, z], me - z + dest, c)
            )
            sends3[-1].start()
        recv3[z, rows] = (cbuf[z, rows] + offset[rows]).astype(BF)

    for h in range(6):
        query_head(h)
    line_totals(0)
    query_head(6)
    line_totals(1)
    query_head(7)
    prefixes(0)
    prefixes(1)

    def finished_head(h):
        state = recv3[h]
        tail = state[144:160].astype(F32)
        norm = jnp.concatenate([tail[9:10], tail[10:11]], 1)
        norm = jnp.broadcast_to(norm, (128, 256)).T[0:FEAT].astype(BF)
        sums = dot(pq[h][:, 0:FEAT], jnp.concatenate([state, norm], 1)) + num[h]
        return (sums[:, :DV] / sums[:, DV:]).astype(BF)

    def arrived_head(i):
        if i == 0:
            return z
        slot = lax.rem(z + Z - i, Z)
        for chunk in range(2):
            rows = rows_of(chunk)
            remote(
                p3.at[i, rows], recv3.at[slot, rows], s3_s.at[chunk, i], s3_r.at[chunk, slot], z_peer(i), c
            ).wait_recv()
        return slot

    def head_rows(h):
        return pl.ds(pl.multiple_of(h * DV, DV), DV)

    order = (0,) + Z_ORDER
    sends_o = []
    for step in range(4):
        heads = [arrived_head(order[2 * step])]
        left = finished_head(heads[0])
        heads.append(arrived_head(order[2 * step + 1]))
        attended = jnp.concatenate([left, finished_head(heads[1])], 1)

        def term(start, n):
            cols = pl.ds(pl.multiple_of(start * HALF + n * TILE, TILE), TILE)
            weights = jnp.concatenate([wob[head_rows(h), cols] for h in heads], 0)
            return dot(attended, weights)

        if step < 3:
            for k, start in enumerate((other, c)):
                for n in range(HALF // TILE):
                    new = term(start, n)
                    acc_out[k, n] = new if step == 0 else acc_out[k, n] + new
        else:
            for n in range(HALF // TILE):
                ttxo[n] = (acc_out[0, n] + term(other, n)).astype(BF)
                sends_o.append(remote(ttxo.at[n], trx.at[n], o_s.at[n], o_r.at[n], me, other))
                sends_o[-1].start()
    squares = jnp.zeros((ROWS, 128), F32)
    for n in range(HALF // TILE):
        mixed = acc_out[1, n] + term(c, n)
        sends_o[n].wait_recv()
        mixed = mixed + trx[n].astype(F32)
        share[n] = mixed
        squares = squares + mixed[:, :128] * mixed[:, :128] + mixed[:, 128:] * mixed[:, 128:]
    sqtx[...] = squares
    send_q = remote(sqtx, sqrx, q_s.at[0], q_r.at[0], me, other)
    send_q.start()
    send_q.wait_recv()
    mean = jnp.sum(sqtx[...] + sqrx[...], 1, keepdims=True) * F32(1.0 / D)
    scale = lax.rsqrt(mean + F32(1e-05))
    for n in range(HALF // TILE):
        gains = jnp.concatenate([gnb[2 * n : 2 * n + 1], gnb[2 * n + 1 : 2 * n + 2]], 1).astype(F32)
        out[:, n * TILE : (n + 1) * TILE] = (share[n] * scale * gains).astype(BF)

    @pl.when(me < Z * PLANE - 1)
    def _():
        for copy in halos:
            copy.wait_send()

    swap.wait_send()
    for copy in sends1 + sends3 + sends_o + [send_q]:
        copy.wait_send()
    for chunk in range(2):
        for i in range(1, PLANE):

            @pl.when(line + i < PLANE)
            def _():
                line_send(chunk, i).wait_send()


def body(tokens, w_query, w_key, w_value, conv_query, conv_key, conv_value, w_out, gain):
    dma = pltpu.SemaphoreType.DMA
    vm = pltpu.VMEM
    return pl.pallas_call(
        kernel,
        out_shape=pltpu.VMEM((ROWS, HALF), BF),
        in_specs=[pl.BlockSpec(memory_space=pl.ANY)] * 9,
        out_specs=pl.BlockSpec(memory_space=pltpu.VMEM),
        scratch_shapes=[
            vm((2, PADDED, HALF), BF), vm((D, 256), BF), vm((D, HALF), BF), vm((HALF, D), BF),
            vm((3, 128), BF), vm((3, 128), BF), vm((3, HALF), BF), vm((8, 128), BF),
            vm((5, PADDED, TILE), F32), vm((PADDED, TILE), F32), vm((128, ROWS), F32), vm((128, ROWS), F32),
            vm((4, ROWS, TILE), BF), vm((HEADS, FEAT, ROWS), BF), vm((HEADS, ROWS, 256), BF),
            vm((HEADS, ROWS, TILE), F32),
            vm((8, FEAT, DV), BF), vm((Z, FEAT, DV), BF), vm((Z, FEAT, DV), F32), vm((FEAT, DV), BF),
            vm((PLANE, FEAT, DV), BF), vm((FEAT, DV), F32), vm((Z, FEAT, DV), BF), vm((Z, FEAT, DV), BF),
            vm((2, 4, ROWS, TILE), F32), vm((4, ROWS, TILE), BF), vm((4, ROWS, TILE), BF), vm((4, ROWS, TILE), F32),
            vm((ROWS, 128), F32), vm((ROWS, 128), F32),
            dma((10,)), dma((1,)), dma((1,)), dma((2,)), dma((2,)), dma((2, 8)), dma((2, 8)),
            dma((2, PLANE)), dma((2, PLANE)), dma((2, 8)), dma((2, 8)), dma((4,)), dma((4,)), dma((1,)), dma((1,)),
        ],
        compiler_params=pltpu.CompilerParams(
            collective_id=0, has_side_effects=True, vmem_limit_bytes=58 * 1024 * 1024
        ),
    )(tokens, w_query, w_key, w_value, conv_query, conv_key, conv_value, w_out, gain.reshape(8, 128))


def solution(mesh):
    return jax.shard_map(
        body,
        mesh=mesh,
        in_specs=(
            P("ctx", "head"),
            P(None, "head"),
            P(None, "head"),
            P(None, "head"),
            P(None, "head"),
            P(None, "head"),
            P(None, "head"),
            P("head", None),
            P("head"),
        ),
        out_specs=P("ctx", "head"),
        check_vma=False,
    )
```

```python
import math

import jax
import jax.numpy as jnp
from jax import lax
from jax.experimental import pallas as pl
from jax.experimental.pallas import tpu as pltpu
from jax.sharding import PartitionSpec as P

D = 2048
HALF = 1024
FD = 16
DV = 128
ROWS = 512
HALO = 16
PADDED = HALO + ROWS
HEADS = 8
FEAT = 160
TILE = 256
SPLIT = 256
Z, Y, X = 8, 4, 4
BF = jnp.bfloat16
F32 = jnp.float32
MESH = pl.DeviceIdType.MESH
PLANE = X * Y
CHUNKS = ((0, 48), (48, 48), (96, 32), (128, 32))
PAIR_ORDER = (2, 1, 3, 0)
Z_ORDER = (4, 3, 5, 2, 6, 1, 7)


def dot(a, b):
    return jnp.dot(a, b, preferred_element_type=F32)


def features(u):
    parts = [u * u * F32(1.0 / math.sqrt(2.0 * FD))]
    for distance in range(1, 8):
        parts.append(u * pltpu.roll(u, FD - distance, 0) * F32(1.0 / math.sqrt(FD)))
    parts.append(u[0:8] * u[8:16] * F32(1.0 / math.sqrt(FD)))
    parts.append(u * F32(FD ** (-0.25)))
    row = lax.broadcasted_iota(jnp.int32, (8, u.shape[1]), 0)
    parts.append(jnp.where(row == 0, F32(1.0), F32(0.0)))
    return jnp.concatenate(parts, 0)


def kernel(
    tok, wq, wk, wv, cq, ck, cv, wo, gn, out,
    xbuf, wqk, wvb, wob, cqb, ckb, cvb, gnb,
    acc, pbuf, qt, kt, vbuf, pk, pq, num,
    loc, recv1, cbuf, ltx, lrx, offset, p3, recv3,
    acc_out, ybuf, yrx, otx, gains,
    lsem, tok_s, tok_r, halo_s, halo_r, s1_s, s1_r, l_s, l_r, s3_s, s3_r, w_s, w_r, g_s, g_r, o_s, o_r, f_s, f_r, ready,
):
    me = lax.axis_index("ctx")
    c = lax.axis_index("head")
    other = 1 - c
    z = lax.rem(me, Z)
    line = lax.div(me, Z)

    def z_peer(i):
        return me - z + lax.rem(z + i, Z)

    def line_peer(i):
        return lax.rem(line + i + PLANE, PLANE) * Z + z

    after = lax.rem(me + 1, Z * Y * X)
    before = lax.rem(me + Z * Y * X - 1, Z * Y * X)

    def remote(src, dst, send, recv, ctx, head):
        return pltpu.make_async_remote_copy(
            src_ref=src, dst_ref=dst, send_sem=send, recv_sem=recv,
            device_id={"ctx": ctx, "head": head}, device_id_type=MESH,
        )

    barrier = pltpu.get_barrier_semaphore()
    def greet(semaphore, ctx, head):
        pl.semaphore_signal(semaphore, inc=1, device_id={"ctx": ctx, "head": head}, device_id_type=MESH)

    greet(barrier, me, other)
    for i in range(1, Z):
        greet(barrier, z_peer(i), c)

    @pl.when(me > 0)
    def _():
        greet(barrier, before, c)
        greet(barrier, before, other)

    for i in range(1, PLANE):

        @pl.when(line + i < PLANE)
        def _():
            greet(barrier, line_peer(i), c)

    mine = pl.ds(pl.multiple_of(c * HALF, HALF), HALF)
    theirs = pl.ds(pl.multiple_of(other * HALF, HALF), HALF)
    tail_rows = pl.ds(HALO, ROWS)
    loads = [
        pltpu.make_async_copy(tok, xbuf.at[c, tail_rows], lsem.at[0]),
        pltpu.make_async_copy(wq, wqk.at[:, pl.ds(0, 128)], lsem.at[1]),
        pltpu.make_async_copy(wk, wqk.at[:, pl.ds(128, 128)], lsem.at[2]),
        pltpu.make_async_copy(wv.at[mine], wvb.at[mine], lsem.at[3]),
        pltpu.make_async_copy(wv.at[theirs], wvb.at[theirs], lsem.at[4]),
        pltpu.make_async_copy(cq, cqb, lsem.at[5]),
        pltpu.make_async_copy(ck, ckb, lsem.at[6]),
        pltpu.make_async_copy(cv, cvb, lsem.at[7]),
        pltpu.make_async_copy(gn, gnb, lsem.at[8]),
        pltpu.make_async_copy(wo, wob.at[mine], lsem.at[9]),
    ]
    for copy in loads:
        copy.start()
    pl.semaphore_wait(barrier, Z + line + jnp.where(me < Z * PLANE - 1, 2, 0))

    last = tok.at[pl.ds(ROWS - HALO, HALO)]
    halos = [
        remote(last, xbuf.at[c, pl.ds(0, HALO)], halo_s.at[0], halo_r.at[c], after, c),
        remote(last, xbuf.at[c, pl.ds(0, HALO)], halo_s.at[1], halo_r.at[c], after, other),
    ]
    swap = remote(tok, xbuf.at[c, tail_rows], tok_s.at[0], tok_r.at[0], me, other)
    swap.start()

    @pl.when(me < Z * PLANE - 1)
    def _():
        for copy in halos:
            copy.start()

    for i in range(1, PLANE):

        @pl.when(line >= i)
        def _():
            greet(ready, line_peer(-i), c)

    def halo_in(half):
        rows = xbuf.at[half, pl.ds(0, HALO)]

        @pl.when(me > 0)
        def _():
            remote(last, rows, halo_s.at[0], halo_r.at[half], before, c).wait_recv()

        @pl.when(me == 0)
        def _():
            rows[...] = jnp.zeros((HALO, HALF), BF)

    halo_in(c)
    for copy in loads[:4]:
        copy.wait()

    def columns(pair):
        return pl.ds(pl.multiple_of(pair * TILE, TILE), TILE)

    pairs = [lax.rem(lax.div(z, 2) + i, 4) for i in PAIR_ORDER]
    acc[0] = dot(xbuf[c], wqk[mine, :])
    for i, pair in enumerate(pairs):
        acc[1 + i] = dot(xbuf[c], wvb[mine, columns(pair)])
    halo_in(other)
    swap.wait_recv()
    weights_out = remote(wo, wob.at[mine], w_s.at[0], w_r.at[0], me, other)
    weights_out.start()
    for copy in loads[4:9]:
        copy.wait()
    gains[c] = gnb[...].astype(F32)
    send_gains = remote(gains.at[c], gains.at[c], g_s.at[0], g_r.at[0], me, other)
    send_gains.start()

    def convolved(taps):
        return (
            taps[0:1] * pbuf[16 : 16 + ROWS, :]
            + taps[1:2] * pbuf[15 : 15 + ROWS, :]
            + taps[2:3] * pbuf[14 : 14 + ROWS, :]
        )

    pbuf[...] = (acc[0] + dot(xbuf[other], wqk[theirs, :])).astype(BF).astype(F32)
    taps = jnp.concatenate([cqb[...].astype(F32), ckb[...].astype(F32)], 1)
    both = convolved(taps).T
    qt[...] = both[0:128]
    kt[...] = both[128:256]

    def key_head(h, value):
        feats = features(kt[pl.ds(pl.multiple_of(h * FD, FD), FD), :]).astype(BF)
        pk[h] = feats
        state = dot(feats, value)
        norm = lax.dot_general(
            jnp.ones((8, ROWS), BF), feats, (((1,), (1,)), ((), ())), preferred_element_type=F32
        )[0:1]
        norm = jnp.concatenate([norm, jnp.zeros((1, 256 - FEAT), F32)], 1)
        row = lax.broadcasted_iota(jnp.int32, (16, DV), 0)
        tail = state[144:160]
        tail = jnp.where(row == 9, norm[:, 0:128], tail)
        tail = jnp.where(row == 10, norm[:, 128:256], tail)
        return jnp.concatenate([state[0:144], tail], 0).astype(BF)

    def rows_of(chunk):
        return pl.ds(*CHUNKS[chunk])

    sends1 = []

    def state_out(slot, dest, chunk):
        rows = rows_of(chunk)
        sends1.append(
            remote(
                loc.at[slot, rows], recv1.at[z, rows], s1_s.at[chunk, slot], s1_r.at[chunk, z], me - z + dest, c
            )
        )
        sends1[-1].start()

    routed = []
    for i, pair in enumerate(pairs):
        pbuf[...] = (acc[1 + i] + dot(xbuf[other], wvb[theirs, columns(pair)])).astype(BF).astype(F32)
        values = convolved(cvb[:, columns(pair)].astype(F32)).astype(BF)
        vbuf[pair] = values
        if PAIR_ORDER[i]:
            for b in range(2):
                slot, dest = 2 * i + b, 2 * pair + b
                loc[slot] = key_head(dest, values[:, b * DV : (b + 1) * DV])
                routed.append((slot, dest))
                state_out(slot, dest, 0)
            for slot, dest in routed[-2:]:
                state_out(slot, dest, 1)
        else:
            half = lax.rem(z, 2)
            slot, dest = 2 * i, 2 * pair + (1 - half)
            loc[slot] = key_head(dest, jnp.where(half == 0, values[:, DV:], values[:, :DV]))
            routed.append((slot, dest))
            state_out(slot, dest, 0)
            state_out(slot, dest, 1)
    for chunk in range(2, len(CHUNKS)):
        for slot, dest in routed:
            state_out(slot, dest, chunk)
    half = lax.rem(z, 2)
    recv1[z] = key_head(z, jnp.where(half == 0, values[:, :DV], values[:, DV:]))

    ones = jnp.ones((ROWS, DV), BF)

    def query_head(h):
        feats = features(qt[h * FD : (h + 1) * FD, :])
        pq[h] = jnp.concatenate([feats, jnp.zeros((256 - FEAT, ROWS), F32)], 0).T.astype(BF)
        value = vbuf[h // 2][:, (h % 2) * DV : (h % 2 + 1) * DV]
        value = jnp.concatenate([value, ones], 1)
        for t in range(ROWS // TILE):
            span = (t + 1) * TILE
            scores = dot(pq[h, t * TILE : span, 0:FEAT], pk[h, :, 0:span])
            row = lax.broadcasted_iota(jnp.int32, (TILE, span), 0) + t * TILE
            col = lax.broadcasted_iota(jnp.int32, (TILE, span), 1)
            scores = jnp.where(row >= col, scores, F32(0.0)).astype(BF)
            num[h, t * TILE : span] = dot(scores, value[0:span])

    def line_send(chunk, i):
        rows = rows_of(chunk)
        return remote(
            ltx.at[rows], lrx.at[i, rows], l_s.at[chunk, i], l_r.at[chunk, i], line_peer(i), c
        )

    def line_totals(chunk):
        rows = rows_of(chunk)
        for i in range(1, Z):
            slot = lax.rem(z + Z - i, Z)
            remote(
                loc.at[0, rows], recv1.at[slot, rows], s1_s.at[chunk, 0], s1_r.at[chunk, slot], z_peer(i), c
            ).wait_recv()
        total = jnp.zeros((CHUNKS[chunk][1], DV), F32)
        for t in range(Z):
            cbuf[t, rows] = total
            total = total + recv1[t, rows].astype(F32)
        ltx[rows] = total.astype(BF)
        if chunk == 0:

            @pl.when(line < PLANE - 1)
            def _():
                pl.semaphore_wait(ready, PLANE - 1 - line)

        for i in range(1, PLANE):

            @pl.when(line + i < PLANE)
            def _():
                line_send(chunk, i).start()

    sends3 = []

    def prefixes(chunk):
        rows = rows_of(chunk)
        offset[rows] = jnp.zeros((CHUNKS[chunk][1], DV), F32)
        for i in range(1, PLANE):

            @pl.when(line >= i)
            def _():
                line_send(chunk, i).wait_recv()
                offset[rows] += lrx[i, rows].astype(F32)

        for i in Z_ORDER:
            dest = lax.rem(z + i, Z)
            p3[i, rows] = (cbuf[dest, rows] + offset[rows]).astype(BF)
            sends3.append(
                remote(p3.at[i, rows], recv3.at[z, rows], s3_s.at[chunk, i], s3_r.at[chunk, z], me - z + dest, c)
            )
            sends3[-1].start()
        recv3[z, rows] = (cbuf[z, rows] + offset[rows]).astype(BF)

    for h in range(6):
        query_head(h)
    line_totals(0)
    query_head(6)
    line_totals(1)
    query_head(7)
    line_totals(2)
    line_totals(3)
    for chunk in range(len(CHUNKS)):
        prefixes(chunk)

    def finished_head(h):
        state = recv3[h]
        tail = state[144:160].astype(F32)
        norm = jnp.concatenate([tail[9:10], tail[10:11]], 1)
        norm = jnp.broadcast_to(norm, (128, 256)).T[0:FEAT].astype(BF)
        sums = dot(pq[h][:, 0:FEAT], jnp.concatenate([state, norm], 1)) + num[h]
        return (sums[:, :DV] / sums[:, DV:]).astype(BF)

    def arrived_head(i):
        if i == 0:
            return z
        slot = lax.rem(z + Z - i, Z)
        for chunk in range(len(CHUNKS)):
            rows = rows_of(chunk)
            remote(
                p3.at[i, rows], recv3.at[slot, rows], s3_s.at[chunk, i], s3_r.at[chunk, slot], z_peer(i), c
            ).wait_recv()
        return slot

    kept = pl.ds(pl.multiple_of(c * SPLIT, SPLIT), SPLIT)
    given = pl.ds(pl.multiple_of(other * SPLIT, SPLIT), SPLIT)
    sends_y = []
    for i in range(HEADS):
        h = arrived_head(((0,) + Z_ORDER)[i])
        lanes = pl.ds(pl.multiple_of(h * DV, DV), DV)
        ybuf[:, lanes] = finished_head(h)
        sends_y.append(remote(ybuf.at[given, lanes], yrx.at[:, lanes], o_s.at[i], o_r.at[i], me, other))
        sends_y[i].start()
    loads[9].wait()
    for n in range(D // TILE):
        acc_out[n] = dot(ybuf[kept, :], wob[mine, n * TILE : (n + 1) * TILE])
    weights_out.wait_recv()
    send_gains.wait_recv()
    for copy in sends_y:
        copy.wait_recv()
    squares = jnp.zeros((SPLIT, 128), F32)
    for n in range(D // TILE):
        pre = acc_out[n] + dot(yrx[...], wob[theirs, n * TILE : (n + 1) * TILE])
        acc_out[n] = pre
        squares = squares + pre[:, :128] * pre[:, :128] + pre[:, 128:] * pre[:, 128:]
    mean = jnp.sum(squares, 1, keepdims=True) * F32(1.0 / D)
    scale = lax.rsqrt(mean + F32(1e-05))

    def normed(core, n):
        gain = jnp.concatenate([gains[core, 2 * n : 2 * n + 1], gains[core, 2 * n + 1 : 2 * n + 2]], 1)
        return (acc_out[core * (HALF // TILE) + n] * scale * gain).astype(BF)

    sends_f = []
    for n in range(HALF // TILE):
        cols = pl.ds(n * TILE, TILE)
        otx[:, cols] = normed(other, n)
        sends_f.append(remote(otx.at[:, cols], out.at[kept, cols], f_s.at[n], f_r.at[n], me, other))
        sends_f[n].start()
    for n in range(HALF // TILE):
        out[kept, n * TILE : (n + 1) * TILE] = normed(c, n)
    for copy in sends_f:
        copy.wait_recv()

    @pl.when(me < Z * PLANE - 1)
    def _():
        for copy in halos:
            copy.wait_send()

    swap.wait_send()
    for copy in sends1 + sends3 + sends_y + sends_f + [weights_out, send_gains]:
        copy.wait_send()
    for chunk in range(len(CHUNKS)):
        for i in range(1, PLANE):

            @pl.when(line + i < PLANE)
            def _():
                line_send(chunk, i).wait_send()


def body(tokens, w_query, w_key, w_value, conv_query, conv_key, conv_value, w_out, gain):
    dma = pltpu.SemaphoreType.DMA
    vm = pltpu.VMEM
    return pl.pallas_call(
        kernel,
        out_shape=pltpu.VMEM((ROWS, HALF), BF),
        in_specs=[pl.BlockSpec(memory_space=pl.ANY)] * 9,
        out_specs=pl.BlockSpec(memory_space=pltpu.VMEM),
        scratch_shapes=[
            vm((2, PADDED, HALF), BF), vm((D, 256), BF), vm((D, HALF), BF), vm((D, D), BF),
            vm((3, 128), BF), vm((3, 128), BF), vm((3, HALF), BF), vm((8, 128), BF),
            vm((5, PADDED, TILE), F32), vm((PADDED, TILE), F32), vm((128, ROWS), F32), vm((128, ROWS), F32),
            vm((4, ROWS, TILE), BF), vm((HEADS, FEAT, ROWS), BF), vm((HEADS, ROWS, 256), BF),
            vm((HEADS, ROWS, TILE), F32),
            vm((8, FEAT, DV), BF), vm((Z, FEAT, DV), BF), vm((Z, FEAT, DV), F32), vm((FEAT, DV), BF),
            vm((PLANE, FEAT, DV), BF), vm((FEAT, DV), F32), vm((Z, FEAT, DV), BF), vm((Z, FEAT, DV), BF),
            vm((8, SPLIT, TILE), F32), vm((ROWS, HALF), BF), vm((SPLIT, HALF), BF), vm((SPLIT, HALF), BF),
            vm((2, 8, 128), F32),
            dma((10,)), dma((1,)), dma((1,)), dma((2,)), dma((2,)), dma((4, 8)), dma((4, 8)),
            dma((4, PLANE)), dma((4, PLANE)), dma((4, 8)), dma((4, 8)), dma((1,)), dma((1,)), dma((1,)), dma((1,)),
            dma((8,)), dma((8,)), dma((4,)), dma((4,)), pltpu.SemaphoreType.REGULAR,
        ],
        compiler_params=pltpu.CompilerParams(
            collective_id=0, has_side_effects=True, vmem_limit_bytes=58 * 1024 * 1024
        ),
    )(tokens, w_query, w_key, w_value, conv_query, conv_key, conv_value, w_out, gain.reshape(8, 128))


def solution(mesh):
    return jax.shard_map(
        body,
        mesh=mesh,
        in_specs=(
            P("ctx", "head"),
            P(None, "head"),
            P(None, "head"),
            P(None, "head"),
            P(None, "head"),
            P(None, "head"),
            P(None, "head"),
            P("head", None),
            P("head"),
        ),
        out_specs=P("ctx", "head"),
        check_vma=False,
    )
```

```python
import math

import jax
import jax.numpy as jnp
from jax import lax
from jax.experimental import pallas as pl
from jax.experimental.pallas import tpu as pltpu
from jax.sharding import PartitionSpec as P

D = 2048
HALF = 1024
FD = 16
DV = 128
ROWS = 512
HALO = 16
PADDED = HALO + ROWS
HEADS = 8
FEAT = 160
TILE = 256
SPLIT = 256
Z, Y, X = 8, 4, 4
BF = jnp.bfloat16
F32 = jnp.float32
MESH = pl.DeviceIdType.MESH
PLANE = X * Y
CHUNKS = ((0, 48), (48, 48), (96, 32), (128, 32))
PAIR_ORDER = (2, 1, 3, 0)
Z_ORDER = (4, 3, 5, 2, 6, 1, 7)


def dot(a, b):
    return jnp.dot(a, b, preferred_element_type=F32)


def features(u):
    parts = [u * u * F32(1.0 / math.sqrt(2.0 * FD))]
    for distance in range(1, 8):
        parts.append(u * pltpu.roll(u, FD - distance, 0) * F32(1.0 / math.sqrt(FD)))
    parts.append(u[0:8] * u[8:16] * F32(1.0 / math.sqrt(FD)))
    parts.append(u * F32(FD ** (-0.25)))
    row = lax.broadcasted_iota(jnp.int32, (8, u.shape[1]), 0)
    parts.append(jnp.where(row == 0, F32(1.0), F32(0.0)))
    return jnp.concatenate(parts, 0)


def kernel(
    tok, wq, wk, wv, cq, ck, cv, wo, gn, out,
    xbuf, wqk, wvb, wob, cqb, ckb, cvb, gnb,
    acc, pqk, pbuf, qt, kt, vbuf, pk, pq, num,
    loc, recv1, cbuf, ltx, lrx, offset, p3, recv3,
    acc_out, ybuf, yrx, otx, gains,
    lsem, tok_s, tok_r, halo_s, halo_r, s1_s, s1_r, l_s, l_r, s3_s, s3_r, w_s, w_r, g_s, g_r, o_s, o_r, f_s, f_r, ready,
):
    me = lax.axis_index("ctx")
    c = lax.axis_index("head")
    other = 1 - c
    z = lax.rem(me, Z)
    line = lax.div(me, Z)

    def z_peer(i):
        return me - z + lax.rem(z + i, Z)

    def line_peer(i):
        return lax.rem(line + i + PLANE, PLANE) * Z + z

    after = lax.rem(me + 1, Z * Y * X)
    before = lax.rem(me + Z * Y * X - 1, Z * Y * X)

    def remote(src, dst, send, recv, ctx, head):
        return pltpu.make_async_remote_copy(
            src_ref=src, dst_ref=dst, send_sem=send, recv_sem=recv,
            device_id={"ctx": ctx, "head": head}, device_id_type=MESH,
        )

    barrier = pltpu.get_barrier_semaphore()
    def greet(semaphore, ctx, head):
        pl.semaphore_signal(semaphore, inc=1, device_id={"ctx": ctx, "head": head}, device_id_type=MESH)

    greet(barrier, me, other)
    for i in range(1, Z):
        greet(barrier, z_peer(i), c)

    @pl.when(me > 0)
    def _():
        greet(barrier, before, c)
        greet(barrier, before, other)

    for i in range(1, PLANE):

        @pl.when(line + i < PLANE)
        def _():
            greet(barrier, line_peer(i), c)

    mine = pl.ds(pl.multiple_of(c * HALF, HALF), HALF)
    theirs = pl.ds(pl.multiple_of(other * HALF, HALF), HALF)
    tail_rows = pl.ds(HALO, ROWS)
    loads = [
        pltpu.make_async_copy(tok, xbuf.at[c, tail_rows], lsem.at[0]),
        pltpu.make_async_copy(wq, wqk.at[:, pl.ds(0, 128)], lsem.at[1]),
        pltpu.make_async_copy(wk, wqk.at[:, pl.ds(128, 128)], lsem.at[2]),
        pltpu.make_async_copy(wv.at[mine], wvb.at[mine], lsem.at[3]),
        pltpu.make_async_copy(wv.at[theirs], wvb.at[theirs], lsem.at[4]),
        pltpu.make_async_copy(cq, cqb, lsem.at[5]),
        pltpu.make_async_copy(ck, ckb, lsem.at[6]),
        pltpu.make_async_copy(cv, cvb, lsem.at[7]),
        pltpu.make_async_copy(gn, gnb, lsem.at[8]),
        pltpu.make_async_copy(wo, wob.at[mine], lsem.at[9]),
    ]
    for copy in loads:
        copy.start()
    pl.semaphore_wait(barrier, Z + line + jnp.where(me < Z * PLANE - 1, 2, 0))

    last = tok.at[pl.ds(ROWS - HALO, HALO)]
    halos = [
        remote(last, xbuf.at[c, pl.ds(0, HALO)], halo_s.at[0], halo_r.at[c], after, c),
        remote(last, xbuf.at[c, pl.ds(0, HALO)], halo_s.at[1], halo_r.at[c], after, other),
    ]
    swap = remote(tok, xbuf.at[c, tail_rows], tok_s.at[0], tok_r.at[0], me, other)
    swap.start()

    @pl.when(me < Z * PLANE - 1)
    def _():
        for copy in halos:
            copy.start()

    for i in range(1, PLANE):

        @pl.when(line >= i)
        def _():
            greet(ready, line_peer(-i), c)

    def halo_in(half):
        rows = xbuf.at[half, pl.ds(0, HALO)]

        @pl.when(me > 0)
        def _():
            remote(last, rows, halo_s.at[0], halo_r.at[half], before, c).wait_recv()

        @pl.when(me == 0)
        def _():
            rows[...] = jnp.zeros((HALO, HALF), BF)

    for copy in loads[:4]:
        copy.wait()

    def columns(pair):
        return pl.ds(pl.multiple_of(pair * TILE, TILE), TILE)

    pairs = [lax.rem(lax.div(z, 2) + i, 4) for i in PAIR_ORDER]
    acc[0] = dot(xbuf[c, HALO:PADDED], wqk[mine, :])
    for i, pair in enumerate(pairs):
        acc[1 + i] = dot(xbuf[c, HALO:PADDED], wvb[mine, columns(pair)])
    halo_in(c)
    halo_in(other)
    swap.wait_recv()
    weights_out = remote(wo, wob.at[mine], w_s.at[0], w_r.at[0], me, other)
    weights_out.start()
    for copy in loads[4:9]:
        copy.wait()
    gains[c] = gnb[...].astype(F32)
    send_gains = remote(gains.at[c], gains.at[c], g_s.at[0], g_r.at[0], me, other)
    send_gains.start()

    def projected(i, own, rest):
        more = dot(xbuf[other], rest)
        first = more[0:HALO] + dot(xbuf[c, 0:HALO], own)
        return jnp.concatenate([first, more[HALO:] + acc[i]], 0).astype(BF).astype(F32)

    pqk[...] = projected(0, wqk[mine, :], wqk[theirs, :])
    taps_k = ckb[...].astype(F32)
    kt[...] = (
        taps_k[0:1] * pqk[16 : 16 + ROWS, 128:256]
        + taps_k[1:2] * pqk[15 : 15 + ROWS, 128:256]
        + taps_k[2:3] * pqk[14 : 14 + ROWS, 128:256]
    ).T

    def key_head(h, value):
        feats = features(kt[pl.ds(pl.multiple_of(h * FD, FD), FD), :]).astype(BF)
        pk[h] = feats
        state = dot(feats, value)
        norm = lax.dot_general(
            jnp.ones((8, ROWS), BF), feats, (((1,), (1,)), ((), ())), preferred_element_type=F32
        )[0:1]
        norm = jnp.concatenate([norm, jnp.zeros((1, 256 - FEAT), F32)], 1)
        row = lax.broadcasted_iota(jnp.int32, (16, DV), 0)
        tail = state[144:160]
        tail = jnp.where(row == 9, norm[:, 0:128], tail)
        tail = jnp.where(row == 10, norm[:, 128:256], tail)
        return jnp.concatenate([state[0:144], tail], 0).astype(BF)

    def rows_of(chunk):
        return pl.ds(*CHUNKS[chunk])

    sends1 = []

    def state_out(slot, dest, chunk):
        rows = rows_of(chunk)
        sends1.append(
            remote(
                loc.at[slot, rows], recv1.at[z, rows], s1_s.at[chunk, slot], s1_r.at[chunk, z], me - z + dest, c
            )
        )
        sends1[-1].start()

    routed = []
    for i, pair in enumerate(pairs):
        pbuf[...] = projected(1 + i, wvb[mine, columns(pair)], wvb[theirs, columns(pair)])
        taps = cvb[:, columns(pair)].astype(F32)
        values = (
            taps[0:1] * pbuf[16 : 16 + ROWS, :]
            + taps[1:2] * pbuf[15 : 15 + ROWS, :]
            + taps[2:3] * pbuf[14 : 14 + ROWS, :]
        ).astype(BF)
        vbuf[pair] = values
        if PAIR_ORDER[i]:
            for b in range(2):
                slot, dest = 2 * i + b, 2 * pair + b
                loc[slot] = key_head(dest, values[:, b * DV : (b + 1) * DV])
                routed.append((slot, dest))
                state_out(slot, dest, 0)
            for slot, dest in routed[-2:]:
                state_out(slot, dest, 1)
        else:
            half = lax.rem(z, 2)
            slot, dest = 2 * i, 2 * pair + (1 - half)
            loc[slot] = key_head(dest, jnp.where(half == 0, values[:, DV:], values[:, :DV]))
            routed.append((slot, dest))
            state_out(slot, dest, 0)
            state_out(slot, dest, 1)
    for chunk in range(2, len(CHUNKS)):
        for slot, dest in routed:
            state_out(slot, dest, chunk)
    half = lax.rem(z, 2)
    recv1[z] = key_head(z, jnp.where(half == 0, values[:, :DV], values[:, DV:]))

    taps_q = cqb[...].astype(F32)
    qt[...] = (
        taps_q[0:1] * pqk[16 : 16 + ROWS, 0:128]
        + taps_q[1:2] * pqk[15 : 15 + ROWS, 0:128]
        + taps_q[2:3] * pqk[14 : 14 + ROWS, 0:128]
    ).T
    ones = jnp.ones((ROWS, DV), BF)

    def query_head(h):
        feats = features(qt[h * FD : (h + 1) * FD, :])
        pq[h] = jnp.concatenate([feats, jnp.zeros((256 - FEAT, ROWS), F32)], 0).T.astype(BF)
        value = vbuf[h // 2][:, (h % 2) * DV : (h % 2 + 1) * DV]
        value = jnp.concatenate([value, ones], 1)
        for t in range(ROWS // TILE):
            span = (t + 1) * TILE
            scores = dot(pq[h, t * TILE : span, 0:FEAT], pk[h, :, 0:span])
            row = lax.broadcasted_iota(jnp.int32, (TILE, span), 0) + t * TILE
            col = lax.broadcasted_iota(jnp.int32, (TILE, span), 1)
            scores = jnp.where(row >= col, scores, F32(0.0)).astype(BF)
            num[h, t * TILE : span] = dot(scores, value[0:span])

    def line_send(chunk, i):
        rows = rows_of(chunk)
        return remote(
            ltx.at[rows], lrx.at[i, rows], l_s.at[chunk, i], l_r.at[chunk, i], line_peer(i), c
        )

    def line_totals(chunk):
        rows = rows_of(chunk)
        for i in range(1, Z):
            slot = lax.rem(z + Z - i, Z)
            remote(
                loc.at[0, rows], recv1.at[slot, rows], s1_s.at[chunk, 0], s1_r.at[chunk, slot], z_peer(i), c
            ).wait_recv()
        total = jnp.zeros((CHUNKS[chunk][1], DV), F32)
        for t in range(Z):
            cbuf[t, rows] = total
            total = total + recv1[t, rows].astype(F32)
        ltx[rows] = total.astype(BF)
        if chunk == 0:

            @pl.when(line < PLANE - 1)
            def _():
                pl.semaphore_wait(ready, PLANE - 1 - line)

        for i in range(1, PLANE):

            @pl.when(line + i < PLANE)
            def _():
                line_send(chunk, i).start()

    sends3 = []

    def prefixes(chunk):
        rows = rows_of(chunk)
        offset[rows] = jnp.zeros((CHUNKS[chunk][1], DV), F32)
        for i in range(1, PLANE):

            @pl.when(line >= i)
            def _():
                line_send(chunk, i).wait_recv()
                offset[rows] += lrx[i, rows].astype(F32)

        for i in Z_ORDER:
            dest = lax.rem(z + i, Z)
            p3[i, rows] = (cbuf[dest, rows] + offset[rows]).astype(BF)
            sends3.append(
                remote(p3.at[i, rows], recv3.at[z, rows], s3_s.at[chunk, i], s3_r.at[chunk, z], me - z + dest, c)
            )
            sends3[-1].start()
        recv3[z, rows] = (cbuf[z, rows] + offset[rows]).astype(BF)

    for h in range(6):
        query_head(h)
    line_totals(0)
    query_head(6)
    line_totals(1)
    query_head(7)
    line_totals(2)
    line_totals(3)
    for chunk in range(len(CHUNKS)):
        prefixes(chunk)

    def finished_head(h):
        state = recv3[h]
        tail = state[144:160].astype(F32)
        norm = jnp.concatenate([tail[9:10], tail[10:11]], 1)
        norm = jnp.broadcast_to(norm, (128, 256)).T[0:FEAT].astype(BF)
        sums = dot(pq[h][:, 0:FEAT], jnp.concatenate([state, norm], 1)) + num[h]
        return (sums[:, :DV] / sums[:, DV:]).astype(BF)

    def arrived_head(i):
        if i == 0:
            return z
        slot = lax.rem(z + Z - i, Z)
        for chunk in range(len(CHUNKS)):
            rows = rows_of(chunk)
            remote(
                p3.at[i, rows], recv3.at[slot, rows], s3_s.at[chunk, i], s3_r.at[chunk, slot], z_peer(i), c
            ).wait_recv()
        return slot

    kept = pl.ds(pl.multiple_of(c * SPLIT, SPLIT), SPLIT)
    given = pl.ds(pl.multiple_of(other * SPLIT, SPLIT), SPLIT)
    sends_y = []
    for i in range(HEADS):
        h = arrived_head(((0,) + Z_ORDER)[i])
        lanes = pl.ds(pl.multiple_of(h * DV, DV), DV)
        ybuf[:, lanes] = finished_head(h)
        sends_y.append(remote(ybuf.at[given, lanes], yrx.at[:, lanes], o_s.at[i], o_r.at[i], me, other))
        sends_y[i].start()
    loads[9].wait()
    for n in range(D // TILE):
        acc_out[n] = dot(ybuf[kept, :], wob[mine, n * TILE : (n + 1) * TILE])
    weights_out.wait_recv()
    send_gains.wait_recv()
    for copy in sends_y:
        copy.wait_recv()
    squares = jnp.zeros((SPLIT, 128), F32)
    for n in range(D // TILE):
        pre = acc_out[n] + dot(yrx[...], wob[theirs, n * TILE : (n + 1) * TILE])
        acc_out[n] = pre
        squares = squares + pre[:, :128] * pre[:, :128] + pre[:, 128:] * pre[:, 128:]
    mean = jnp.sum(squares, 1, keepdims=True) * F32(1.0 / D)
    scale = lax.rsqrt(mean + F32(1e-05))

    def normed(core, n):
        gain = jnp.concatenate([gains[core, 2 * n : 2 * n + 1], gains[core, 2 * n + 1 : 2 * n + 2]], 1)
        return (acc_out[core * (HALF // TILE) + n] * scale * gain).astype(BF)

    sends_f = []
    for n in range(HALF // TILE):
        cols = pl.ds(n * TILE, TILE)
        otx[:, cols] = normed(other, n)
        sends_f.append(remote(otx.at[:, cols], out.at[kept, cols], f_s.at[n], f_r.at[n], me, other))
        sends_f[n].start()
    for n in range(HALF // TILE):
        out[kept, n * TILE : (n + 1) * TILE] = normed(c, n)
    for copy in sends_f:
        copy.wait_recv()

    @pl.when(me < Z * PLANE - 1)
    def _():
        for copy in halos:
            copy.wait_send()

    swap.wait_send()
    for copy in sends1 + sends3 + sends_y + sends_f + [weights_out, send_gains]:
        copy.wait_send()
    for chunk in range(len(CHUNKS)):
        for i in range(1, PLANE):

            @pl.when(line + i < PLANE)
            def _():
                line_send(chunk, i).wait_send()


def body(tokens, w_query, w_key, w_value, conv_query, conv_key, conv_value, w_out, gain):
    dma = pltpu.SemaphoreType.DMA
    vm = pltpu.VMEM
    return pl.pallas_call(
        kernel,
        out_shape=pltpu.VMEM((ROWS, HALF), BF),
        in_specs=[pl.BlockSpec(memory_space=pl.ANY)] * 9,
        out_specs=pl.BlockSpec(memory_space=pltpu.VMEM),
        scratch_shapes=[
            vm((2, PADDED, HALF), BF), vm((D, 256), BF), vm((D, HALF), BF), vm((D, D), BF),
            vm((3, 128), BF), vm((3, 128), BF), vm((3, HALF), BF), vm((8, 128), BF),
            vm((5, ROWS, TILE), F32), vm((PADDED, TILE), F32), vm((PADDED, TILE), F32), vm((128, ROWS), F32), vm((128, ROWS), F32),
            vm((4, ROWS, TILE), BF), vm((HEADS, FEAT, ROWS), BF), vm((HEADS, ROWS, 256), BF),
            vm((HEADS, ROWS, TILE), F32),
            vm((8, FEAT, DV), BF), vm((Z, FEAT, DV), BF), vm((Z, FEAT, DV), F32), vm((FEAT, DV), BF),
            vm((PLANE, FEAT, DV), BF), vm((FEAT, DV), F32), vm((Z, FEAT, DV), BF), vm((Z, FEAT, DV), BF),
            vm((8, SPLIT, TILE), F32), vm((ROWS, HALF), BF), vm((SPLIT, HALF), BF), vm((SPLIT, HALF), BF),
            vm((2, 8, 128), F32),
            dma((10,)), dma((1,)), dma((1,)), dma((2,)), dma((2,)), dma((4, 8)), dma((4, 8)),
            dma((4, PLANE)), dma((4, PLANE)), dma((4, 8)), dma((4, 8)), dma((1,)), dma((1,)), dma((1,)), dma((1,)),
            dma((8,)), dma((8,)), dma((4,)), dma((4,)), pltpu.SemaphoreType.REGULAR,
        ],
        compiler_params=pltpu.CompilerParams(
            collective_id=0, has_side_effects=True, vmem_limit_bytes=58 * 1024 * 1024
        ),
    )(tokens, w_query, w_key, w_value, conv_query, conv_key, conv_value, w_out, gain.reshape(8, 128))


def solution(mesh):
    return jax.shard_map(
        body,
        mesh=mesh,
        in_specs=(
            P("ctx", "head"),
            P(None, "head"),
            P(None, "head"),
            P(None, "head"),
            P(None, "head"),
            P(None, "head"),
            P(None, "head"),
            P("head", None),
            P("head"),
        ),
        out_specs=P("ctx", "head"),
        check_vma=False,
    )
```
